32 devices in a mesh: gr: 8 (over y, x, core), gc: 4 (over z).
Axes of the slice: x: 2, y: 2, z: 4, core: 2. Of those that a mesh axis runs over, the one named last changes fastest.
Arguments:
- border: bfloat16 [24, 768, 2048], P('gc', None, 'gr'), may hold values from -1 to 1
- row_scale: float32 [24, 768], P('gc'), may hold values from 0.1 to 10
- block_pick: int32 [24, 16], replicated, may hold values from 0 to 3
- given_diag: float32 [8192], replicated, may hold values from 0.5 to 4
Outputs:
- factored: float32 [8192, 8192], P('gr', 'gc')
The draws below stay inside these ranges and needn't reach their ends.
All inputs are finite; a program needn't handle non-finite values.
Results may differ from the reference program's by a relative error of at most 0.00097.
Values may be sent and summed in bfloat16 or wider, within the bound.
A program may use at most 128 MiB of HBM per device.

```python
import math
import jax
import jax.numpy as jnp
from jax import lax

N = 8192
BLK = 128
NWIN = 16
WSPAN = 4
R = 768
PW = 256
PANELS = 2
SCEN = 24


def draw_border(key, part):
    keys = jax.random.split(jax.random.fold_in(key, 17), 3)
    width = NWIN * BLK
    spread = (R * SCEN / WSPAN) ** (-0.5)
    noise = jnp.clip(jax.random.normal(keys[0], (SCEN, R, width), jnp.float32), -4.0, 4.0)
    loads = jnp.clip(jax.random.normal(keys[1], (SCEN, R, 3), jnp.float32), -3.0, 3.0)
    factors = jnp.clip(jax.random.normal(keys[2], (SCEN, 3, width), jnp.float32), -3.0, 3.0)
    lowpart = loads[:, :, 0:1] * factors[:, 0:1, :]
    lowpart = lowpart + loads[:, :, 1:2] * factors[:, 1:2, :]
    lowpart = lowpart + loads[:, :, 2:3] * factors[:, 2:3, :]
    values = jnp.clip(spread * (noise + 0.5 * lowpart), -1.0, 1.0)
    return values.astype(jnp.bfloat16)


def touch_ends(entries, stream_key, least, high):
    extent = entries.shape
    spot = [jax.random.randint(jax.random.fold_in(stream_key, axis), (), 0, extent[axis]) for axis in range(len(extent))]
    entries = entries.at[tuple(spot)].set(least)
    longest = extent.index(max(extent))
    spot[longest] = (spot[longest] + 1) % extent[longest]
    return entries.at[tuple(spot)].set(high)


def block_levels(key, extent, cuts, low, high):
    def one(position, parts):
        steps = jax.random.uniform(jax.random.fold_in(jax.random.fold_in(key, 6), position), (parts,), jnp.float32, low / len(cuts), high / len(cuts))
        return jnp.repeat(jnp.exp(steps), extent[position] // parts).reshape((-1,) + (1,) * (len(extent) - position - 1))

    loudness = one(*cuts[0])
    for cut in cuts[1:]:
        loudness = loudness * one(*cut)
    return loudness


def setup_inputs(seed: int = 0) -> dict:
    key_list = jax.random.split(jax.random.key(seed), 5)
    border = draw_border(jax.random.fold_in(key_list[4], 71), 0)
    row_scale = jnp.clip(jnp.exp(math.log(10.0) - 4.6051702 * jax.random.uniform(key_list[1], (SCEN, R), jnp.float32) ** block_levels(key_list[1], (SCEN, R), ((0, 4),), -0.2, 0.2)), 0.1, 10.0)
    block_pick = touch_ends(jax.random.randint(key_list[2], (SCEN, NWIN), 0, WSPAN), jax.random.fold_in(key_list[2], 1), 0, WSPAN - 1).astype(jnp.int32)
    given_diag = jnp.clip(jnp.exp(jax.random.uniform(key_list[3], (N,), jnp.float32, math.log(0.5), math.log(4.0))), 0.5, 4.0)
    return {"border": border, "row_scale": row_scale, "block_pick": block_pick, "given_diag": given_diag}


def reference(border, row_scale, block_pick, given_diag):
    window_base = jnp.arange(NWIN, dtype=jnp.int32) * WSPAN
    within = jnp.arange(BLK, dtype=jnp.int32)

    def add_scenario(total, item):
        slab, scale_row, pick_row = item
        scaled = (jnp.sqrt(scale_row)[:, None] * slab.astype(jnp.float32)).astype(jnp.bfloat16)
        wide = scaled.astype(jnp.float32)
        gram = jnp.dot(wide.T.astype(jnp.float32), wide.astype(jnp.float32), precision=lax.Precision.HIGHEST, preferred_element_type=jnp.float32)
        blocks = window_base + pick_row.astype(jnp.int32)
        columns = (blocks[:, None] * BLK + within[None, :]).reshape(-1).astype(jnp.int32)
        total = total.at[columns[:, None], columns[None, :]].add(gram)
        return (total, None)
    start = jnp.diag(given_diag.astype(jnp.float32))
    factored, _ = lax.scan(add_scenario, start, (border, row_scale, block_pick))
    row_global = jnp.arange(N, dtype=jnp.int32)
    for panel_index in range(PANELS):
        first_col = panel_index * PW
        past_col = first_col + PW
        chol_block = jnp.linalg.cholesky(factored[first_col:past_col, first_col:past_col])
        column_part = factored[:, first_col:past_col]
        solved = jax.scipy.linalg.solve_triangular(chol_block, column_part.T, lower=True).T
        solved = jnp.where((row_global >= past_col)[:, None], solved, 0.0)
        solved = solved.at[first_col:past_col].set(chol_block)
        product = jnp.dot(solved.astype(jnp.float32), solved.T.astype(jnp.float32), precision=lax.Precision.HIGHEST, preferred_element_type=jnp.float32)
        trailing = (row_global >= past_col)[:, None] & (row_global >= past_col)[None, :]
        factored = jnp.where(trailing, factored - product, factored)
        factored = factored.at[:, first_col:past_col].set(solved)
        factored = factored.at[first_col:past_col, past_col:].set(0.0)
    return factored
```

```python
import functools

import jax
import jax.numpy as jnp
from jax import lax
from jax.experimental import pallas as pl
from jax.experimental.pallas import tpu as pltpu
from jax.sharding import PartitionSpec as P

N = 8192
BLK = 128
NWIN = 16
WSPAN = 4
HEAD = 512
MESH = pl.DeviceIdType.MESH


def ring_swap(p):
    return p + ((p // 2) % 2) * (1 - 2 * (p % 2))


def gather_kernel(dims, scaled, rows, cols, head, own_sem, zrecv, zsend, recv, rsend, ssend):
    grid_rows, grid_cols, roots, parts, group = dims
    chips = grid_rows // 2
    units = grid_cols * parts
    me = lax.axis_index("gr")
    z = lax.axis_index("gc")
    core = lax.rem(me, 2)
    pos = ring_swap(me // 2)
    sibling = me + 1 - 2 * core
    ahead = ring_swap(lax.rem(pos + 1, chips)) * 2 + core
    behind = ring_swap(lax.rem(pos + chips - 1, chips)) * 2 + core
    has_up = z < grid_cols - 1
    has_down = z > 0

    barrier = pltpu.get_barrier_semaphore()
    for other in (sibling, ahead, behind):
        pl.semaphore_signal(barrier, inc=1, device_id=(other, z), device_id_type=MESH)

    @pl.when(has_up)
    def _():
        pl.semaphore_signal(barrier, inc=1, device_id=(me, z + 1), device_id_type=MESH)

    @pl.when(has_down)
    def _():
        pl.semaphore_signal(barrier, inc=1, device_id=(me, z - 1), device_id_type=MESH)

    own = pltpu.make_async_copy(
        scaled, rows.at[pl.ds(z * parts * group, parts * group)], own_sem
    )
    own.start()
    pl.semaphore_wait(barrier, 3 + has_up.astype(jnp.int32) + has_down.astype(jnp.int32))
    own.wait()

    def zcopy(unit, up):
        where = pl.ds(unit * group, group)
        return pltpu.make_async_remote_copy(
            src_ref=rows.at[where],
            dst_ref=rows.at[where],
            send_sem=zsend.at[1 if up else 0, unit],
            recv_sem=zrecv.at[unit],
            device_id=(me, z + 1 if up else z - 1),
            device_id_type=MESH,
        )

    def target(k, unit):
        where = pl.ds(unit * group, group)
        return head.at[where] if k == roots else cols.at[k, where]

    def source(k, unit):
        where = pl.ds(unit * group, group)
        return rows.at[where, :, pl.ds(0, BLK)] if k == roots else rows.at[where]

    def ring_copy(k, unit, src, forward):
        return pltpu.make_async_remote_copy(
            src_ref=src,
            dst_ref=target(k, unit),
            send_sem=rsend.at[k, unit],
            recv_sem=recv.at[k, unit],
            device_id=(ahead if forward else behind, z),
            device_id_type=MESH,
        )

    def sibling_copy(k, unit, src):
        return pltpu.make_async_remote_copy(
            src_ref=src,
            dst_ref=target(k, unit),
            send_sem=ssend.at[k, unit],
            recv_sem=recv.at[k, unit],
            device_id=(sibling, z),
            device_id_type=MESH,
        )

    def own_copy(k, unit):
        return pltpu.make_async_copy(source(k, unit), target(k, unit), recv.at[k, unit])

    def stream(k):
        root = z * roots + k if k < roots else 0 * z
        on_ring = core == lax.rem(root, 2)
        d = lax.rem(pos - ring_swap(root // 2) + chips, chips)
        return on_ring, d, lax.rem(chips - d, chips)

    streams = [stream(k) for k in range(roots + 1)]

    def send_along(k, unit, hop, forward):
        @pl.when(hop == 0)
        def _():
            own_copy(k, unit).start()
            ring_copy(k, unit, source(k, unit), forward).start()
            sibling_copy(k, unit, source(k, unit)).start()

        @pl.when(hop > 0)
        def _():
            ring_copy(k, unit, target(k, unit), forward).wait_recv()

            @pl.when(hop < chips - 1)
            def _():
                ring_copy(k, unit, target(k, unit), forward).start()

            sibling_copy(k, unit, target(k, unit)).start()

    def step(i, carry):
        t, s = i // parts, lax.rem(i, parts)
        low, high = z - t, z + t

        @pl.when(jnp.logical_and(t < grid_cols, low >= 0))
        def _():
            @pl.when(t > 0)
            def _():
                zcopy(low * parts + s, True).wait_recv()

            @pl.when(has_up)
            def _():
                zcopy(low * parts + s, True).start()

        @pl.when(jnp.logical_and(t < grid_cols, high < grid_cols))
        def _():
            @pl.when(t > 0)
            def _():
                zcopy(high * parts + s, False).wait_recv()

            @pl.when(has_down)
            def _():
                zcopy(high * parts + s, False).start()

        for forward in (True, False):
            for k in range(roots + 1):
                on_ring, d_ahead, d_behind = streams[k]
                hop = d_ahead if forward else d_behind
                slot = i - hop
                t2, s2 = slot // parts, lax.rem(slot, parts)
                good = jnp.logical_and(slot >= 0, slot < units)
                good = jnp.logical_and(good, lax.rem(slot, 2) == (0 if forward else 1))
                good = jnp.logical_and(good, on_ring)

                @pl.when(jnp.logical_and(good, z - t2 >= 0))
                def _():
                    send_along(k, (z - t2) * parts + s2, hop, forward)

                other = jnp.logical_and(t2 > 0, z + t2 < grid_cols)

                @pl.when(jnp.logical_and(good, other))
                def _():
                    send_along(k, (z + t2) * parts + s2, hop, forward)

        return carry

    lax.fori_loop(0, units + chips - 1, step, 0)

    def finish(unit, carry):
        c, s = unit // parts, lax.rem(unit, parts)

        @pl.when(jnp.logical_and(c <= z, has_up))
        def _():
            zcopy(unit, True).wait_send()

        @pl.when(jnp.logical_and(c >= z, has_down))
        def _():
            zcopy(unit, False).wait_send()

        slot = jnp.where(c > z, c - z, z - c) * parts + s
        even = lax.rem(slot, 2) == 0
        for k in range(roots + 1):
            on_ring, d_ahead, d_behind = streams[k]
            hop = jnp.where(even, d_ahead, d_behind)

            @pl.when(on_ring)
            def _():
                @pl.when(hop < chips - 1)
                def _():
                    ring_copy(k, unit, target(k, unit), True).wait_send()

                sibling_copy(k, unit, target(k, unit)).wait_send()

                @pl.when(hop == 0)
                def _():
                    own_copy(k, unit).wait()

            @pl.when(jnp.logical_not(on_ring))
            def _():
                sibling_copy(k, unit, target(k, unit)).wait_recv()

        return carry

    lax.fori_loop(0, units, finish, 0)


def gather(scaled, grid_rows, grid_cols):
    here, depth, width = scaled.shape
    roots = grid_rows // grid_cols
    parts = here if grid_cols <= 4 else 1
    group = here // parts
    units = grid_cols * parts
    total = here * grid_cols
    dims = (grid_rows, grid_cols, roots, parts, group)
    dma = pltpu.SemaphoreType.DMA
    return pl.pallas_call(
        functools.partial(gather_kernel, dims),
        out_shape=(
            jax.ShapeDtypeStruct((total, depth, width), scaled.dtype),
            jax.ShapeDtypeStruct((roots, total, depth, width), scaled.dtype),
            jax.ShapeDtypeStruct((total, depth, BLK), scaled.dtype),
        ),
        in_specs=[pl.BlockSpec(memory_space=pl.ANY)],
        out_specs=[pl.BlockSpec(memory_space=pl.ANY)] * 3,
        scratch_shapes=[
            dma,
            dma((units,)),
            dma((2, units)),
            dma((roots + 1, units)),
            dma((roots + 1, units)),
            dma((roots + 1, units)),
        ],
        compiler_params=pltpu.CompilerParams(collective_id=0, has_side_effects=True),
        name="gather",
    )(scaled)


def tdot(a, b):
    return lax.dot_general(a, b, (((0,), (0,)), ((), ())), preferred_element_type=jnp.float32)


def assemble_kernel(roots, row_pick, col_pick, head_pick, rows, cols, head, acc, left, top, corner):
    s = pl.program_id(0)

    @pl.when(s == 0)
    def _():
        acc[...] = jnp.zeros_like(acc)
        left[...] = jnp.zeros_like(left)
        top[...] = jnp.zeros_like(top)
        corner[...] = jnp.zeros_like(corner)

    row_wins = rows.shape[2] // BLK
    xr = rows[0]
    xh = head[0]

    def place(pick):
        return pl.ds(pl.multiple_of(pick * BLK, BLK), BLK)

    def spot(win, pick):
        return pl.ds(pl.multiple_of(win * WSPAN * BLK + pick * BLK, BLK), BLK)

    at_head = place(head_pick[s])
    corner[at_head, at_head] += tdot(xh, xh)
    g = tdot(xr, xh)
    for a in range(row_wins):
        left[spot(a, row_pick[s, a]), at_head] += g[a * BLK : (a + 1) * BLK]
    for k in range(roots):
        xc = cols[k, 0]
        g = tdot(xr, xc)
        h = tdot(xh, xc)
        for b in range(row_wins):
            here = spot(k * row_wins + b, col_pick[s, k * row_wins + b])
            part = slice(b * BLK, (b + 1) * BLK)
            top[at_head, here] += h[:, part]
            for a in range(row_wins):
                acc[spot(a, row_pick[s, a]), here] += g[a * BLK : (a + 1) * BLK, part]


def assemble(row_pick, col_pick, head_pick, rows, cols, head, local_rows, local_cols):
    total, depth, width = rows.shape
    roots = cols.shape[0]
    f32 = jnp.float32
    whole = lambda s, *_: (0, 0)
    grid_spec = pltpu.PrefetchScalarGridSpec(
        num_scalar_prefetch=3,
        grid=(total,),
        in_specs=[
            pl.BlockSpec((1, depth, width), lambda s, *_: (s, 0, 0)),
            pl.BlockSpec((roots, 1, depth, width), lambda s, *_: (0, s, 0, 0)),
            pl.BlockSpec((1, depth, BLK), lambda s, *_: (s, 0, 0)),
        ],
        out_specs=[
            pl.BlockSpec((local_rows, local_cols), whole),
            pl.BlockSpec((local_rows, HEAD), whole),
            pl.BlockSpec((HEAD, local_cols), whole),
            pl.BlockSpec((HEAD, HEAD), whole),
        ],
    )
    return pl.pallas_call(
        functools.partial(assemble_kernel, roots),
        grid_spec=grid_spec,
        out_shape=(
            jax.ShapeDtypeStruct((local_rows, local_cols), f32),
            jax.ShapeDtypeStruct((local_rows, HEAD), f32),
            jax.ShapeDtypeStruct((HEAD, local_cols), f32),
            jax.ShapeDtypeStruct((HEAD, HEAD), f32),
        ),
        compiler_params=pltpu.CompilerParams(vmem_limit_bytes=56 * 1024 * 1024),
        name="assemble",
    )(row_pick, col_pick, head_pick, rows, cols, head)


def full_dot(a, b, dims):
    return lax.dot_general(
        a, b, (dims, ((), ())), precision=lax.Precision.HIGHEST, preferred_element_type=jnp.float32
    )


def factor_kernel(corner, diag, lower, inverse, work, aug):
    blocks = HEAD // BLK
    ri = lax.broadcasted_iota(jnp.int32, (HEAD, HEAD), 0)
    ci = lax.broadcasted_iota(jnp.int32, (HEAD, HEAD), 1)
    work[...] = corner[...] + jnp.where(ri == ci, diag[...], 0.0)
    lower[...] = jnp.zeros_like(lower)
    inverse[...] = jnp.zeros_like(inverse)
    rb = lax.broadcasted_iota(jnp.int32, (BLK, BLK), 0)
    cb = lax.broadcasted_iota(jnp.int32, (BLK, BLK), 1)
    lane = lax.broadcasted_iota(jnp.int32, (1, BLK), 1)
    for kb in range(blocks):
        lo, hi = kb * BLK, (kb + 1) * BLK
        aug[:, :BLK] = work[lo:hi, lo:hi]
        aug[:, BLK:] = jnp.where(rb == cb, 1.0, 0.0)

        def eliminate(j, carry):
            row = aug[pl.ds(j, 1), :]
            pivot = jnp.sum(jnp.where(lane == j, row[:, :BLK], 0.0), axis=1, keepdims=True)
            scale = lax.rsqrt(pivot)
            block = aug[...]
            col = jnp.sum(jnp.where(cb == j, block[:, :BLK], 0.0), axis=1, keepdims=True)
            done = rb[:, :1]
            unit = row * scale
            factor = jnp.where(done > j, col * scale, 0.0)
            block = block - factor * unit
            aug[...] = jnp.where(done == j, unit, block)
            return carry

        lax.fori_loop(0, BLK, eliminate, 0)
        upper = jnp.where(cb >= rb, aug[:, :BLK], 0.0)
        inv = jnp.where(cb <= rb, aug[:, BLK:], 0.0)
        lower[lo:hi, lo:hi] = upper.T
        inverse[lo:hi, lo:hi] = inv
        if hi < HEAD:
            below = full_dot(work[hi:, lo:hi], inv, ((1,), (1,)))
            lower[hi:, lo:hi] = below
            work[hi:, hi:] = work[hi:, hi:] - full_dot(below, below, ((1,), (1,)))
        if kb > 0:
            mix = full_dot(lower[lo:hi, :lo], inverse[:lo, :lo], ((1,), (0,)))
            inverse[lo:hi, :lo] = -full_dot(inv, mix, ((1,), (0,)))


def factor(corner, diag):
    shape = jax.ShapeDtypeStruct((HEAD, HEAD), jnp.float32)
    return pl.pallas_call(
        factor_kernel,
        out_shape=(shape, shape),
        scratch_shapes=[
            pltpu.VMEM((HEAD, HEAD), jnp.float32),
            pltpu.VMEM((BLK, 2 * BLK), jnp.float32),
        ],
        compiler_params=pltpu.CompilerParams(vmem_limit_bytes=32 * 1024 * 1024),
        name="factor",
    )(corner, diag.reshape(1, HEAD))


def split(x):
    high = x.astype(jnp.bfloat16)
    return high, (x - high.astype(jnp.float32)).astype(jnp.bfloat16)


def three_dot(a, b, dims):
    dot = functools.partial(
        lax.dot_general, dimension_numbers=(dims, ((), ())), preferred_element_type=jnp.float32
    )
    return dot(a[0], b[0]) + (dot(a[0], b[1]) + dot(a[1], b[0]))


def update_kernel(tile, place, acc, left, top, lower, inverse, diag, out, top_high, top_low):
    i = pl.program_id(0)
    row_zero, col_zero = place[0], place[1]
    inv = split(inverse[...])

    @pl.when(i == 0)
    def _():
        wide = 512
        for c in range(top.shape[1] // wide):
            at = slice(c * wide, (c + 1) * wide)
            high, low = split(three_dot(inv, split(top[:, at]), ((1,), (0,))))
            top_high[:, at] = high
            top_low[:, at] = low

    panel = three_dot(split(left[...]), inv, ((1,), (1,)))
    first = row_zero + i * tile
    product = three_dot(split(panel), (top_high[...], top_low[...]), ((1,), (0,)))
    cols = out.shape[1]
    r = first + lax.broadcasted_iota(jnp.int32, (tile, cols), 0)
    c = col_zero + lax.broadcasted_iota(jnp.int32, (tile, cols), 1)
    out[...] = acc[...] + jnp.where(r == c, diag[...], 0.0) - product

    @pl.when(first < HEAD)
    def _():
        out[...] = jnp.zeros_like(out)

    @pl.when(col_zero == 0)
    def _():
        out[:, :HEAD] = panel

        @pl.when(first < HEAD)
        def _():
            out[:, :HEAD] = lower[pl.ds(pl.multiple_of(first, tile), tile), :]


def update(place, acc, left, top, lower, inverse, diag):
    rows, cols = acc.shape
    tile = 256
    whole = lambda i, *_: (0, 0)
    grid_spec = pltpu.PrefetchScalarGridSpec(
        num_scalar_prefetch=1,
        grid=(rows // tile,),
        in_specs=[
            pl.BlockSpec((tile, cols), lambda i, *_: (i, 0)),
            pl.BlockSpec((tile, HEAD), lambda i, *_: (i, 0)),
            pl.BlockSpec((HEAD, cols), whole),
            pl.BlockSpec((HEAD, HEAD), whole),
            pl.BlockSpec((HEAD, HEAD), whole),
            pl.BlockSpec((1, cols), whole),
        ],
        out_specs=pl.BlockSpec((tile, cols), lambda i, *_: (i, 0)),
        scratch_shapes=[
            pltpu.VMEM((HEAD, cols), jnp.bfloat16),
            pltpu.VMEM((HEAD, cols), jnp.bfloat16),
        ],
    )
    return pl.pallas_call(
        functools.partial(update_kernel, tile),
        grid_spec=grid_spec,
        out_shape=jax.ShapeDtypeStruct((rows, cols), jnp.float32),
        compiler_params=pltpu.CompilerParams(vmem_limit_bytes=56 * 1024 * 1024),
        name="update",
    )(place, acc, left, top, lower, inverse, diag.reshape(1, cols))


def body(border, row_scale, block_pick, given_diag):
    grid_rows = lax.axis_size("gr")
    grid_cols = lax.axis_size("gc")
    row_index = lax.axis_index("gr")
    col_index = lax.axis_index("gc")
    row_windows = NWIN // grid_rows
    col_windows = NWIN // grid_cols
    local_rows = N // grid_rows
    local_cols = N // grid_cols
    scaled = (jnp.sqrt(row_scale)[:, :, None] * border.astype(jnp.float32)).astype(jnp.bfloat16)
    rows, cols, head = gather(scaled, grid_rows, grid_cols)
    row_pick = lax.dynamic_slice_in_dim(block_pick, row_index * row_windows, row_windows, 1)
    col_pick = lax.dynamic_slice_in_dim(block_pick, col_index * col_windows, col_windows, 1)
    acc, left, top, corner = assemble(
        row_pick, col_pick, block_pick[:, 0], rows, cols, head, local_rows, local_cols
    )
    lower, inverse = factor(corner, given_diag[:HEAD])
    place = jnp.stack([row_index * local_rows, col_index * local_cols]).astype(jnp.int32)
    diag_here = lax.dynamic_slice_in_dim(given_diag, col_index * local_cols, local_cols, 0)
    return update(place, acc, left, top, lower, inverse, diag_here)


def solution(mesh):
    in_specs = (P("gc", None, "gr"), P("gc", None), P(), P())
    out_specs = P("gr", "gc")
    return jax.shard_map(body, mesh=mesh, in_specs=in_specs, out_specs=out_specs, check_vma=False)
```

```python
import functools

import jax
import jax.numpy as jnp
from jax import lax
from jax.experimental import pallas as pl
from jax.experimental.pallas import tpu as pltpu
from jax.sharding import PartitionSpec as P

N = 8192
BLK = 128
NWIN = 16
WSPAN = 4
HEAD = 512
MESH = pl.DeviceIdType.MESH


def ring_swap(p):
    return p + ((p // 2) % 2) * (1 - 2 * (p % 2))


def gather_kernel(dims, scaled, rows, cols, head, own_sem, zrecv, zsend, recv, rsend, ssend):
    grid_rows, grid_cols, roots, parts, group = dims
    chips = grid_rows // 2
    units = grid_cols * parts
    me = lax.axis_index("gr")
    z = lax.axis_index("gc")
    core = lax.rem(me, 2)
    pos = ring_swap(me // 2)
    sibling = me + 1 - 2 * core
    ahead = ring_swap(lax.rem(pos + 1, chips)) * 2 + core
    behind = ring_swap(lax.rem(pos + chips - 1, chips)) * 2 + core
    has_up = z < grid_cols - 1
    has_down = z > 0

    barrier = pltpu.get_barrier_semaphore()
    for other in (sibling, ahead, behind):
        pl.semaphore_signal(barrier, inc=1, device_id=(other, z), device_id_type=MESH)

    @pl.when(has_up)
    def _():
        pl.semaphore_signal(barrier, inc=1, device_id=(me, z + 1), device_id_type=MESH)

    @pl.when(has_down)
    def _():
        pl.semaphore_signal(barrier, inc=1, device_id=(me, z - 1), device_id_type=MESH)

    own = pltpu.make_async_copy(
        scaled, rows.at[pl.ds(z * parts * group, parts * group)], own_sem
    )
    own.start()
    pl.semaphore_wait(barrier, 3 + has_up.astype(jnp.int32) + has_down.astype(jnp.int32))
    def mine(s):
        return scaled.at[pl.ds(s * group, group)]

    def zcopy(unit, up, src=None):
        where = pl.ds(unit * group, group)
        return pltpu.make_async_remote_copy(
            src_ref=rows.at[where] if src is None else src,
            dst_ref=rows.at[where],
            send_sem=zsend.at[1 if up else 0, unit],
            recv_sem=zrecv.at[unit],
            device_id=(me, z + 1 if up else z - 1),
            device_id_type=MESH,
        )

    def target(k, unit):
        where = pl.ds(unit * group, group)
        return head.at[where] if k == roots else cols.at[k, where]

    def narrow(k, ref):
        return ref.at[:, :, pl.ds(0, BLK)] if k == roots else ref

    def ring_copy(k, unit, src, forward):
        return pltpu.make_async_remote_copy(
            src_ref=src,
            dst_ref=target(k, unit),
            send_sem=rsend.at[k, unit],
            recv_sem=recv.at[k, unit],
            device_id=(ahead if forward else behind, z),
            device_id_type=MESH,
        )

    def sibling_copy(k, unit, src):
        return pltpu.make_async_remote_copy(
            src_ref=src,
            dst_ref=target(k, unit),
            send_sem=ssend.at[k, unit],
            recv_sem=recv.at[k, unit],
            device_id=(sibling, z),
            device_id_type=MESH,
        )

    def stream(k):
        root = z * roots + k if k < roots else 0 * z
        on_ring = core == lax.rem(root, 2)
        d = lax.rem(pos - ring_swap(root // 2) + chips, chips)
        return on_ring, d, lax.rem(chips - d, chips)

    streams = [stream(k) for k in range(roots + 1)]

    def send_along(k, unit, hop, forward, own_part):
        def both(src):
            ring_copy(k, unit, src, forward).start()
            sibling_copy(k, unit, src).start()

        @pl.when(hop == 0)
        def _():
            here = unit // parts == z

            @pl.when(here)
            def _():
                both(narrow(k, mine(own_part)))

            @pl.when(jnp.logical_not(here))
            def _():
                both(narrow(k, rows.at[pl.ds(unit * group, group)]))

        @pl.when(hop > 0)
        def _():
            ring_copy(k, unit, target(k, unit), forward).wait_recv()

            @pl.when(hop < chips - 1)
            def _():
                ring_copy(k, unit, target(k, unit), forward).start()

            sibling_copy(k, unit, target(k, unit)).start()

    def step(i, carry):
        t, s = i // parts, lax.rem(i, parts)
        low, high = z - t, z + t

        @pl.when(t == 0)
        def _():
            @pl.when(has_up)
            def _():
                zcopy(z * parts + s, True, mine(s)).start()

            @pl.when(has_down)
            def _():
                zcopy(z * parts + s, False, mine(s)).start()

        later = jnp.logical_and(t > 0, t < grid_cols)

        @pl.when(jnp.logical_and(later, low >= 0))
        def _():
            zcopy(low * parts + s, True).wait_recv()

            @pl.when(has_up)
            def _():
                zcopy(low * parts + s, True).start()

        @pl.when(jnp.logical_and(later, high < grid_cols))
        def _():
            zcopy(high * parts + s, False).wait_recv()

            @pl.when(has_down)
            def _():
                zcopy(high * parts + s, False).start()

        for forward in (True, False):
            for k in range(roots + 1):
                on_ring, d_ahead, d_behind = streams[k]
                hop = d_ahead if forward else d_behind
                slot = i - hop
                t2, s2 = slot // parts, lax.rem(slot, parts)
                good = jnp.logical_and(slot >= 0, slot < units)
                good = jnp.logical_and(good, lax.rem(slot, 2) == (0 if forward else 1))
                good = jnp.logical_and(good, on_ring)

                @pl.when(jnp.logical_and(good, z - t2 >= 0))
                def _():
                    send_along(k, (z - t2) * parts + s2, hop, forward, s2)

                other = jnp.logical_and(t2 > 0, z + t2 < grid_cols)

                @pl.when(jnp.logical_and(good, other))
                def _():
                    send_along(k, (z + t2) * parts + s2, hop, forward, s2)

        return carry

    lax.fori_loop(0, units + chips - 1, step, 0)

    def finish(unit, carry):
        c, s = unit // parts, lax.rem(unit, parts)

        @pl.when(jnp.logical_and(c <= z, has_up))
        def _():
            zcopy(unit, True).wait_send()

        @pl.when(jnp.logical_and(c >= z, has_down))
        def _():
            zcopy(unit, False).wait_send()

        slot = jnp.where(c > z, c - z, z - c) * parts + s
        even = lax.rem(slot, 2) == 0
        for k in range(roots + 1):
            on_ring, d_ahead, d_behind = streams[k]
            hop = jnp.where(even, d_ahead, d_behind)

            @pl.when(on_ring)
            def _():
                @pl.when(hop < chips - 1)
                def _():
                    ring_copy(k, unit, target(k, unit), True).wait_send()

                sibling_copy(k, unit, target(k, unit)).wait_send()

            @pl.when(jnp.logical_not(on_ring))
            def _():
                sibling_copy(k, unit, target(k, unit)).wait_recv()

        return carry

    lax.fori_loop(0, units, finish, 0)
    own.wait()


def gather(scaled, grid_rows, grid_cols):
    here, depth, width = scaled.shape
    roots = grid_rows // grid_cols
    parts = here if grid_cols <= 4 else 1
    group = here // parts
    units = grid_cols * parts
    total = here * grid_cols
    dims = (grid_rows, grid_cols, roots, parts, group)
    dma = pltpu.SemaphoreType.DMA
    return pl.pallas_call(
        functools.partial(gather_kernel, dims),
        out_shape=(
            jax.ShapeDtypeStruct((total, depth, width), scaled.dtype),
            jax.ShapeDtypeStruct((roots, total, depth, width), scaled.dtype),
            jax.ShapeDtypeStruct((total, depth, BLK), scaled.dtype),
        ),
        in_specs=[pl.BlockSpec(memory_space=pl.ANY)],
        out_specs=[pl.BlockSpec(memory_space=pl.ANY)] * 3,
        scratch_shapes=[
            dma,
            dma((units,)),
            dma((2, units)),
            dma((roots + 1, units)),
            dma((roots + 1, units)),
            dma((roots + 1, units)),
        ],
        compiler_params=pltpu.CompilerParams(collective_id=0, has_side_effects=True),
        name="gather",
    )(scaled)


def full_dot(a, b, dims):
    return lax.dot_general(
        a, b, (dims, ((), ())), precision=lax.Precision.HIGHEST, preferred_element_type=jnp.float32
    )


def split(x):
    high = x.astype(jnp.bfloat16)
    return high, (x - high.astype(jnp.float32)).astype(jnp.bfloat16)


def three_dot(a, b, dims):
    dot = functools.partial(
        lax.dot_general, dimension_numbers=(dims, ((), ())), preferred_element_type=jnp.float32
    )
    return dot(a[0], b[0]) + (dot(a[0], b[1]) + dot(a[1], b[0]))


STEP = 4


def eliminate(jj, aug):
    rb = lax.broadcasted_iota(jnp.int32, (BLK, BLK), 0)
    cb = lax.broadcasted_iota(jnp.int32, (BLK, BLK), 1)
    lane = lax.broadcasted_iota(jnp.int32, (1, BLK), 1)
    j = jj * STEP
    block = aug[...]
    rows = [aug[pl.ds(j + a, 1), :] for a in range(STEP)]
    pick = lambda x, at, n: jnp.sum(jnp.where(at == n, x, 0.0), axis=1, keepdims=True)
    cols = [pick(block[:, :BLK], cb, j + a) for a in range(STEP)]
    low = [[None] * STEP for _ in range(STEP)]
    inv = [None] * STEP
    for a in range(STEP):
        for b in range(a + 1):
            v = pick(rows[b][:, :BLK], lane, j + a)
            for c in range(b):
                v = v - low[b][c] * low[a][c]
            if a == b:
                inv[a] = lax.rsqrt(v)
            else:
                low[a][b] = v * inv[b]
    done = rb[:, :1]
    units, factors = [], []
    for a in range(STEP):
        u, f = rows[a], cols[a]
        for b in range(a):
            u = u - low[a][b] * units[b]
            f = f - low[a][b] * factors[b]
        units.append(u * inv[a])
        factors.append(f * inv[a])
    for a in range(STEP):
        block = block - jnp.where(done >= j + STEP, factors[a], 0.0) * units[a]
    aug[...] = block
    for a in range(STEP):
        aug[pl.ds(j + a, 1), :] = units[a]


def factor(work, lower, inverse, aug):
    blocks = HEAD // BLK
    lower[...] = jnp.zeros_like(lower)
    inverse[...] = jnp.zeros_like(inverse)
    rb = lax.broadcasted_iota(jnp.int32, (BLK, BLK), 0)
    cb = lax.broadcasted_iota(jnp.int32, (BLK, BLK), 1)
    for kb in range(blocks):
        lo, hi = kb * BLK, (kb + 1) * BLK
        aug[:, :BLK] = work[lo:hi, lo:hi]
        aug[:, BLK:] = jnp.where(rb == cb, 1.0, 0.0)

        def turn(jj, carry):
            eliminate(jj, aug)
            return carry

        lax.fori_loop(0, BLK // STEP, turn, 0)
        upper = jnp.where(cb >= rb, aug[:, :BLK], 0.0)
        inv = jnp.where(cb <= rb, aug[:, BLK:], 0.0)
        lower[lo:hi, lo:hi] = upper.T
        inverse[lo:hi, lo:hi] = inv
        if hi < HEAD:
            below = full_dot(work[hi:, lo:hi], inv, ((1,), (1,)))
            lower[hi:, lo:hi] = below
            work[hi:, hi:] = work[hi:, hi:] - full_dot(below, below, ((1,), (1,)))
        if kb > 0:
            mix = full_dot(lower[lo:hi, :lo], inverse[:lo, :lo], ((1,), (0,)))
            inverse[lo:hi, :lo] = -full_dot(inv, mix, ((1,), (0,)))


def finish_kernel(
    roots, place, row_pick, col_pick, head_pick, rows, cols, head, diag_head, diag_cols, out,
    left, top, corner, lower, inverse, aug, lhs, rhs, top_high, top_low,
):
    s = pl.program_id(0)
    row_zero, col_zero, own_stream, own_head = place[0], place[1], place[2], place[3]
    width = rows.shape[2]
    row_wins = width // BLK

    @pl.when(s == 0)
    def _():
        out[...] = jnp.zeros_like(out)
        left[...] = jnp.zeros_like(left)
        top[...] = jnp.zeros_like(top)
        r = lax.broadcasted_iota(jnp.int32, (HEAD, HEAD), 0)
        c = lax.broadcasted_iota(jnp.int32, (HEAD, HEAD), 1)
        corner[...] = jnp.where(r == c, diag_head[...], 0.0)

    lhs[:, :width] = rows[0]
    for k in range(roots):
        part = slice(k * width, (k + 1) * width)

        @pl.when(own_stream == k)
        def _():
            rhs[:, part] = rows[0]

        @pl.when(own_stream != k)
        def _():
            rhs[:, part] = cols[k, 0]

    @pl.when(own_head == 1)
    def _():
        lhs[:, width:] = rows[0, :, :BLK]
        rhs[:, roots * width :] = rows[0, :, :BLK]

    @pl.when(own_head == 0)
    def _():
        lhs[:, width:] = head[0]
        rhs[:, roots * width :] = head[0]

    gram = lax.dot_general(
        lhs[...], rhs[...], (((0,), (0,)), ((), ())), preferred_element_type=jnp.float32
    )

    def spot(win, pick):
        return pl.ds(pl.multiple_of(win * WSPAN * BLK + pick * BLK, BLK), BLK)

    at_head = spot(0, head_pick[s])
    cut = lambda a, b: gram[a * BLK : (a + 1) * BLK, b * BLK : (b + 1) * BLK]
    col_wins = roots * row_wins
    corner[at_head, at_head] += cut(row_wins, col_wins)
    for a in range(row_wins):
        left[spot(a, row_pick[s, a]), at_head] += cut(a, col_wins)
    for b in range(col_wins):
        here = spot(b, col_pick[s, b])
        top[at_head, here] += cut(row_wins, b)
        for a in range(row_wins):
            out[spot(a, row_pick[s, a]), here] += cut(a, b)

    @pl.when(s == pl.num_programs(0) - 1)
    def _():
        factor(corner, lower, inverse, aug)
        inv = split(inverse[...])
        n_rows, n_cols = out.shape
        wide = 512
        for c in range(n_cols // wide):
            at = slice(c * wide, (c + 1) * wide)
            top_high[:, at], top_low[:, at] = split(
                three_dot(inv, split(top[:, at]), ((1,), (0,)))
            )
        tile = 256

        def strip(i, carry):
            at = pl.ds(pl.multiple_of(i * tile, tile), tile)
            panel = three_dot(split(left[at, :]), inv, ((1,), (1,)))
            first = row_zero + i * tile

            @pl.when(first >= HEAD)
            def _():
                product = three_dot(split(panel), (top_high[...], top_low[...]), ((1,), (0,)))
                r = first + lax.broadcasted_iota(jnp.int32, (tile, n_cols), 0)
                c = col_zero + lax.broadcasted_iota(jnp.int32, (tile, n_cols), 1)
                out[at, :] = out[at, :] + jnp.where(r == c, diag_cols[...], 0.0) - product

                @pl.when(col_zero == 0)
                def _():
                    out[at, :HEAD] = panel

            @pl.when(first < HEAD)
            def _():
                out[at, :] = jnp.zeros((tile, n_cols), jnp.float32)

                @pl.when(col_zero == 0)
                def _():
                    out[at, :HEAD] = lower[pl.ds(pl.multiple_of(first, tile), tile), :]

            return carry

        lax.fori_loop(0, n_rows // tile, strip, 0)


def finish(place, row_pick, col_pick, head_pick, rows, cols, head, diag_head, diag_cols, n_rows, n_cols):
    total, depth, width = rows.shape
    roots = cols.shape[0]
    f32, bf16 = jnp.float32, jnp.bfloat16
    whole = lambda s, *_: (0, 0)
    grid_spec = pltpu.PrefetchScalarGridSpec(
        num_scalar_prefetch=4,
        grid=(total,),
        in_specs=[
            pl.BlockSpec((1, depth, width), lambda s, *_: (s, 0, 0)),
            pl.BlockSpec((roots, 1, depth, width), lambda s, *_: (0, s, 0, 0)),
            pl.BlockSpec((1, depth, BLK), lambda s, *_: (s, 0, 0)),
            pl.BlockSpec((1, HEAD), whole),
            pl.BlockSpec((1, n_cols), whole),
        ],
        out_specs=pl.BlockSpec((n_rows, n_cols), whole),
        scratch_shapes=[
            pltpu.VMEM((n_rows, HEAD), f32),
            pltpu.VMEM((HEAD, n_cols), f32),
            pltpu.VMEM((HEAD, HEAD), f32),
            pltpu.VMEM((HEAD, HEAD), f32),
            pltpu.VMEM((HEAD, HEAD), f32),
            pltpu.VMEM((BLK, 2 * BLK), f32),
            pltpu.VMEM((depth, width + BLK), bf16),
            pltpu.VMEM((depth, roots * width + BLK), bf16),
            pltpu.VMEM((HEAD, n_cols), bf16),
            pltpu.VMEM((HEAD, n_cols), bf16),
        ],
    )
    return pl.pallas_call(
        functools.partial(finish_kernel, roots),
        grid_spec=grid_spec,
        out_shape=jax.ShapeDtypeStruct((n_rows, n_cols), f32),
        compiler_params=pltpu.CompilerParams(vmem_limit_bytes=56 * 1024 * 1024),
        name="finish",
    )(
        place, row_pick, col_pick, head_pick, rows, cols, head,
        diag_head.reshape(1, HEAD), diag_cols.reshape(1, n_cols),
    )


def body(border, row_scale, block_pick, given_diag):
    grid_rows = lax.axis_size("gr")
    grid_cols = lax.axis_size("gc")
    row_index = lax.axis_index("gr")
    col_index = lax.axis_index("gc")
    row_windows = NWIN // grid_rows
    col_windows = NWIN // grid_cols
    local_rows = N // grid_rows
    local_cols = N // grid_cols
    scaled = (jnp.sqrt(row_scale)[:, :, None] * border.astype(jnp.float32)).astype(jnp.bfloat16)
    rows, cols, head = gather(scaled, grid_rows, grid_cols)
    row_pick = lax.dynamic_slice_in_dim(block_pick, row_index * row_windows, row_windows, 1)
    col_pick = lax.dynamic_slice_in_dim(block_pick, col_index * col_windows, col_windows, 1)
    roots = grid_rows // grid_cols
    own_stream = row_index - col_index * roots
    place = jnp.stack(
        [
            row_index * local_rows,
            col_index * local_cols,
            own_stream,
            (row_index == 0).astype(jnp.int32),
        ]
    ).astype(jnp.int32)
    diag_cols = lax.dynamic_slice_in_dim(given_diag, col_index * local_cols, local_cols, 0)
    return finish(
        place, row_pick, col_pick, block_pick[:, 0], rows, cols, head,
        given_diag[:HEAD], diag_cols, local_rows, local_cols,
    )


def solution(mesh):
    in_specs = (P("gc", None, "gr"), P("gc", None), P(), P())
    out_specs = P("gr", "gc")
    return jax.shard_map(body, mesh=mesh, in_specs=in_specs, out_specs=out_specs, check_vma=False)
```

```python
import functools

import jax
import jax.numpy as jnp
from jax import lax
from jax.experimental import pallas as pl
from jax.experimental.pallas import tpu as pltpu
from jax.sharding import PartitionSpec as P

N = 8192
BLK = 128
NWIN = 16
WSPAN = 4
HEAD = 512
MESH = pl.DeviceIdType.MESH
PIECES = 2


def ring_swap(p):
    return p + ((p // 2) % 2) * (1 - 2 * (p % 2))


def gather_kernel(dims, scaled, rows, cols, head, own_sem, zrecv, zsend, recv, rsend, ssend):
    grid_rows, grid_cols, roots, parts, group = dims
    chips = grid_rows // 2
    units = grid_cols * parts
    me = lax.axis_index("gr")
    z = lax.axis_index("gc")
    core = lax.rem(me, 2)
    pos = ring_swap(me // 2)
    sibling = me + 1 - 2 * core
    ahead = ring_swap(lax.rem(pos + 1, chips)) * 2 + core
    behind = ring_swap(lax.rem(pos + chips - 1, chips)) * 2 + core
    has_up = z < grid_cols - 1
    has_down = z > 0

    barrier = pltpu.get_barrier_semaphore()
    for other in (sibling, ahead, behind):
        pl.semaphore_signal(barrier, inc=1, device_id=(other, z), device_id_type=MESH)

    @pl.when(has_up)
    def _():
        pl.semaphore_signal(barrier, inc=1, device_id=(me, z + 1), device_id_type=MESH)

    @pl.when(has_down)
    def _():
        pl.semaphore_signal(barrier, inc=1, device_id=(me, z - 1), device_id_type=MESH)

    own = pltpu.make_async_copy(
        scaled, rows.at[pl.ds(z * parts * group, parts * group)], own_sem
    )
    own.start()
    pl.semaphore_wait(barrier, 3 + has_up.astype(jnp.int32) + has_down.astype(jnp.int32))
    def mine(s):
        return scaled.at[pl.ds(s * group, group)]

    def zcopy(unit, up, src=None):
        where = pl.ds(unit * group, group)
        return pltpu.make_async_remote_copy(
            src_ref=rows.at[where] if src is None else src,
            dst_ref=rows.at[where],
            send_sem=zsend.at[1 if up else 0, unit],
            recv_sem=zrecv.at[unit],
            device_id=(me, z + 1 if up else z - 1),
            device_id_type=MESH,
        )

    def target(k, unit):
        where = pl.ds(unit * group, group)
        return head.at[where] if k == roots else cols.at[k, where]

    def narrow(k, ref):
        return ref.at[:, :, pl.ds(0, BLK)] if k == roots else ref

    def ring_copy(k, unit, src, forward):
        return pltpu.make_async_remote_copy(
            src_ref=src,
            dst_ref=target(k, unit),
            send_sem=rsend.at[k, unit],
            recv_sem=recv.at[k, unit],
            device_id=(ahead if forward else behind, z),
            device_id_type=MESH,
        )

    def sibling_copy(k, unit, src):
        return pltpu.make_async_remote_copy(
            src_ref=src,
            dst_ref=target(k, unit),
            send_sem=ssend.at[k, unit],
            recv_sem=recv.at[k, unit],
            device_id=(sibling, z),
            device_id_type=MESH,
        )

    def stream(k):
        root = z * roots + k if k < roots else 0 * z
        on_ring = core == lax.rem(root, 2)
        d = lax.rem(pos - ring_swap(root // 2) + chips, chips)
        return on_ring, d, lax.rem(chips - d, chips)

    streams = [stream(k) for k in range(roots + 1)]

    def send_along(k, unit, hop, forward, own_part):
        def both(src):
            ring_copy(k, unit, src, forward).start()
            sibling_copy(k, unit, src).start()

        @pl.when(hop == 0)
        def _():
            here = unit // parts == z

            @pl.when(here)
            def _():
                both(narrow(k, mine(own_part)))

            @pl.when(jnp.logical_not(here))
            def _():
                both(narrow(k, rows.at[pl.ds(unit * group, group)]))

        @pl.when(hop > 0)
        def _():
            ring_copy(k, unit, target(k, unit), forward).wait_recv()

            @pl.when(hop < chips - 1)
            def _():
                ring_copy(k, unit, target(k, unit), forward).start()

            sibling_copy(k, unit, target(k, unit)).start()

    def step(i, carry):
        t, s = i // parts, lax.rem(i, parts)
        low, high = z - t, z + t

        @pl.when(t == 0)
        def _():
            @pl.when(has_up)
            def _():
                zcopy(z * parts + s, True, mine(s)).start()

            @pl.when(has_down)
            def _():
                zcopy(z * parts + s, False, mine(s)).start()

        later = jnp.logical_and(t > 0, t < grid_cols)

        @pl.when(jnp.logical_and(later, low >= 0))
        def _():
            zcopy(low * parts + s, True).wait_recv()

            @pl.when(has_up)
            def _():
                zcopy(low * parts + s, True).start()

        @pl.when(jnp.logical_and(later, high < grid_cols))
        def _():
            zcopy(high * parts + s, False).wait_recv()

            @pl.when(has_down)
            def _():
                zcopy(high * parts + s, False).start()

        for forward in (True, False):
            for k in range(roots + 1):
                on_ring, d_ahead, d_behind = streams[k]
                hop = d_ahead if forward else d_behind
                slot = i - hop
                t2, s2 = slot // parts, lax.rem(slot, parts)
                good = jnp.logical_and(slot >= 0, slot < units)
                good = jnp.logical_and(good, lax.rem(slot, 2) == (0 if forward else 1))
                good = jnp.logical_and(good, on_ring)

                @pl.when(jnp.logical_and(good, z - t2 >= 0))
                def _():
                    send_along(k, (z - t2) * parts + s2, hop, forward, s2)

                other = jnp.logical_and(t2 > 0, z + t2 < grid_cols)

                @pl.when(jnp.logical_and(good, other))
                def _():
                    send_along(k, (z + t2) * parts + s2, hop, forward, s2)

        return carry

    lax.fori_loop(0, units + chips - 1, step, 0)

    def finish(unit, carry):
        c, s = unit // parts, lax.rem(unit, parts)

        @pl.when(jnp.logical_and(c <= z, has_up))
        def _():
            zcopy(unit, True).wait_send()

        @pl.when(jnp.logical_and(c >= z, has_down))
        def _():
            zcopy(unit, False).wait_send()

        slot = jnp.where(c > z, c - z, z - c) * parts + s
        even = lax.rem(slot, 2) == 0
        for k in range(roots + 1):
            on_ring, d_ahead, d_behind = streams[k]
            hop = jnp.where(even, d_ahead, d_behind)

            @pl.when(on_ring)
            def _():
                @pl.when(hop < chips - 1)
                def _():
                    ring_copy(k, unit, target(k, unit), True).wait_send()

                sibling_copy(k, unit, target(k, unit)).wait_send()

            @pl.when(jnp.logical_not(on_ring))
            def _():
                sibling_copy(k, unit, target(k, unit)).wait_recv()

        return carry

    lax.fori_loop(0, units, finish, 0)
    own.wait()


def gather(scaled, grid_rows, grid_cols):
    here, depth, width = scaled.shape
    roots = grid_rows // grid_cols
    parts = here if grid_cols <= 4 else 1
    group = here // parts
    units = grid_cols * parts
    total = here * grid_cols
    dims = (grid_rows, grid_cols, roots, parts, group)
    dma = pltpu.SemaphoreType.DMA
    return pl.pallas_call(
        functools.partial(gather_kernel, dims),
        out_shape=(
            jax.ShapeDtypeStruct((total, depth, width), scaled.dtype),
            jax.ShapeDtypeStruct((roots, total, depth, width), scaled.dtype),
            jax.ShapeDtypeStruct((total, depth, BLK), scaled.dtype),
        ),
        in_specs=[pl.BlockSpec(memory_space=pl.ANY)],
        out_specs=[pl.BlockSpec(memory_space=pl.ANY)] * 3,
        scratch_shapes=[
            dma,
            dma((units,)),
            dma((2, units)),
            dma((roots + 1, units)),
            dma((roots + 1, units)),
            dma((roots + 1, units)),
        ],
        compiler_params=pltpu.CompilerParams(collective_id=0, has_side_effects=True),
        name="gather",
    )(scaled)


def full_dot(a, b, dims):
    return lax.dot_general(
        a, b, (dims, ((), ())), precision=lax.Precision.HIGHEST, preferred_element_type=jnp.float32
    )


def split(x):
    high = x.astype(jnp.bfloat16)
    return high, (x - high.astype(jnp.float32)).astype(jnp.bfloat16)


def three_dot(a, b, dims):
    dot = functools.partial(
        lax.dot_general, dimension_numbers=(dims, ((), ())), preferred_element_type=jnp.float32
    )
    return dot(a[0], b[0]) + (dot(a[0], b[1]) + dot(a[1], b[0]))


STEP = 4


def eliminate(jj, aug):
    rb = lax.broadcasted_iota(jnp.int32, (BLK, BLK), 0)
    cb = lax.broadcasted_iota(jnp.int32, (BLK, BLK), 1)
    lane = lax.broadcasted_iota(jnp.int32, (1, BLK), 1)
    j = jj * STEP
    block = aug[...]
    rows = [aug[pl.ds(j + a, 1), :] for a in range(STEP)]
    pick = lambda x, at, n: jnp.sum(jnp.where(at == n, x, 0.0), axis=1, keepdims=True)
    cols = [pick(block[:, :BLK], cb, j + a) for a in range(STEP)]
    low = [[None] * STEP for _ in range(STEP)]
    inv = [None] * STEP
    for a in range(STEP):
        for b in range(a + 1):
            v = pick(rows[b][:, :BLK], lane, j + a)
            for c in range(b):
                v = v - low[b][c] * low[a][c]
            if a == b:
                inv[a] = lax.rsqrt(v)
            else:
                low[a][b] = v * inv[b]
    done = rb[:, :1]
    units, factors = [], []
    for a in range(STEP):
        u, f = rows[a], cols[a]
        for b in range(a):
            u = u - low[a][b] * units[b]
            f = f - low[a][b] * factors[b]
        units.append(u * inv[a])
        factors.append(f * inv[a])
    for a in range(STEP):
        block = block - jnp.where(done >= j + STEP, factors[a], 0.0) * units[a]
    aug[...] = block
    for a in range(STEP):
        aug[pl.ds(j + a, 1), :] = units[a]


def factor(work, lower, inverse, aug):
    blocks = HEAD // BLK
    lower[...] = jnp.zeros_like(lower)
    inverse[...] = jnp.zeros_like(inverse)
    rb = lax.broadcasted_iota(jnp.int32, (BLK, BLK), 0)
    cb = lax.broadcasted_iota(jnp.int32, (BLK, BLK), 1)
    for kb in range(blocks):
        lo, hi = kb * BLK, (kb + 1) * BLK
        aug[:, :BLK] = work[lo:hi, lo:hi]
        aug[:, BLK:] = jnp.where(rb == cb, 1.0, 0.0)

        def turn(jj, carry):
            eliminate(jj, aug)
            return carry

        lax.fori_loop(0, BLK // STEP, turn, 0)
        upper = jnp.where(cb >= rb, aug[:, :BLK], 0.0)
        inv = jnp.where(cb <= rb, aug[:, BLK:], 0.0)
        lower[lo:hi, lo:hi] = upper.T
        inverse[lo:hi, lo:hi] = inv
        if hi < HEAD:
            below = full_dot(work[hi:, lo:hi], inv, ((1,), (1,)))
            lower[hi:, lo:hi] = below
            work[hi:, hi:] = work[hi:, hi:] - full_dot(below, below, ((1,), (1,)))
        if kb > 0:
            mix = full_dot(lower[lo:hi, :lo], inverse[:lo, :lo], ((1,), (0,)))
            inverse[lo:hi, :lo] = -full_dot(inv, mix, ((1,), (0,)))


def finish_kernel(
    roots, place, row_pick, col_pick, head_pick, rows, cols, head, diag_head, diag_cols, out,
    left, top, corner, lower, inverse, aug, lhs, rhs, top_high, top_low,
):
    s = pl.program_id(0)
    row_zero, col_zero, own_stream, own_head = place[0], place[1], place[2], place[3]
    width = rows.shape[2]
    row_wins = width // BLK

    @pl.when(s == 0)
    def _():
        out[...] = jnp.zeros_like(out)
        left[...] = jnp.zeros_like(left)
        top[...] = jnp.zeros_like(top)
        r = lax.broadcasted_iota(jnp.int32, (HEAD, HEAD), 0)
        c = lax.broadcasted_iota(jnp.int32, (HEAD, HEAD), 1)
        corner[...] = jnp.where(r == c, diag_head[...], 0.0)

    lhs[:, :width] = rows[0]
    for k in range(roots):
        part = slice(k * width, (k + 1) * width)

        @pl.when(own_stream == k)
        def _():
            rhs[:, part] = rows[0]

        @pl.when(own_stream != k)
        def _():
            rhs[:, part] = cols[k, 0]

    @pl.when(own_head == 1)
    def _():
        lhs[:, width:] = rows[0, :, :BLK]
        rhs[:, roots * width :] = rows[0, :, :BLK]

    @pl.when(own_head == 0)
    def _():
        lhs[:, width:] = head[0]
        rhs[:, roots * width :] = head[0]

    gram = lax.dot_general(
        lhs[...], rhs[...], (((0,), (0,)), ((), ())), preferred_element_type=jnp.float32
    )

    def spot(win, pick):
        return pl.ds(pl.multiple_of(win * WSPAN * BLK + pick * BLK, BLK), BLK)

    at_head = spot(0, head_pick[s])
    cut = lambda a, b: gram[a * BLK : (a + 1) * BLK, b * BLK : (b + 1) * BLK]
    col_wins = roots * row_wins
    corner[at_head, at_head] += cut(row_wins, col_wins)
    for a in range(row_wins):
        left[spot(a, row_pick[s, a]), at_head] += cut(a, col_wins)
    for b in range(col_wins):
        here = spot(b, col_pick[s, b])
        top[at_head, here] += cut(row_wins, b)
        for a in range(row_wins):
            out[spot(a, row_pick[s, a]), here] += cut(a, b)

    @pl.when(s == pl.num_programs(0) - 1)
    def _():
        factor(corner, lower, inverse, aug)
        inv = split(inverse[...])
        n_rows, n_cols = out.shape
        wide = 512
        for c in range(n_cols // wide):
            at = slice(c * wide, (c + 1) * wide)
            top_high[:, at], top_low[:, at] = split(
                three_dot(inv, split(top[:, at]), ((1,), (0,)))
            )
        tile = 256

        def strip(i, carry):
            at = pl.ds(pl.multiple_of(i * tile, tile), tile)
            panel = three_dot(split(left[at, :]), inv, ((1,), (1,)))
            first = row_zero + i * tile

            @pl.when(first >= HEAD)
            def _():
                product = three_dot(split(panel), (top_high[...], top_low[...]), ((1,), (0,)))
                r = first + lax.broadcasted_iota(jnp.int32, (tile, n_cols), 0)
                c = col_zero + lax.broadcasted_iota(jnp.int32, (tile, n_cols), 1)
                out[at, :] = out[at, :] + jnp.where(r == c, diag_cols[...], 0.0) - product

                @pl.when(col_zero == 0)
                def _():
                    out[at, :HEAD] = panel

            @pl.when(first < HEAD)
            def _():
                out[at, :] = jnp.zeros((tile, n_cols), jnp.float32)

                @pl.when(col_zero == 0)
                def _():
                    out[at, :HEAD] = lower[pl.ds(pl.multiple_of(first, tile), tile), :]

            return carry

        lax.fori_loop(0, n_rows // tile, strip, 0)


def finish(place, row_pick, col_pick, head_pick, rows, cols, head, diag_head, diag_cols, n_rows, n_cols):
    total, depth, width = rows.shape
    roots = cols.shape[0]
    f32, bf16 = jnp.float32, jnp.bfloat16
    whole = lambda s, *_: (0, 0)
    grid_spec = pltpu.PrefetchScalarGridSpec(
        num_scalar_prefetch=4,
        grid=(total,),
        in_specs=[
            pl.BlockSpec((1, depth, width), lambda s, *_: (s, 0, 0)),
            pl.BlockSpec((roots, 1, depth, width), lambda s, *_: (0, s, 0, 0)),
            pl.BlockSpec((1, depth, BLK), lambda s, *_: (s, 0, 0)),
            pl.BlockSpec((1, HEAD), whole),
            pl.BlockSpec((1, n_cols), whole),
        ],
        out_specs=pl.BlockSpec((n_rows, n_cols), whole),
        scratch_shapes=[
            pltpu.VMEM((n_rows, HEAD), f32),
            pltpu.VMEM((HEAD, n_cols), f32),
            pltpu.VMEM((HEAD, HEAD), f32),
            pltpu.VMEM((HEAD, HEAD), f32),
            pltpu.VMEM((HEAD, HEAD), f32),
            pltpu.VMEM((BLK, 2 * BLK), f32),
            pltpu.VMEM((depth, width + BLK), bf16),
            pltpu.VMEM((depth, roots * width + BLK), bf16),
            pltpu.VMEM((HEAD, n_cols), bf16),
            pltpu.VMEM((HEAD, n_cols), bf16),
        ],
    )
    return pl.pallas_call(
        functools.partial(finish_kernel, roots),
        grid_spec=grid_spec,
        out_shape=jax.ShapeDtypeStruct((n_rows, n_cols), f32),
        compiler_params=pltpu.CompilerParams(vmem_limit_bytes=56 * 1024 * 1024),
        name="finish",
    )(
        place, row_pick, col_pick, head_pick, rows, cols, head,
        diag_head.reshape(1, HEAD), diag_cols.reshape(1, n_cols),
    )


def body(border, row_scale, block_pick, given_diag):
    grid_rows = lax.axis_size("gr")
    grid_cols = lax.axis_size("gc")
    row_index = lax.axis_index("gr")
    col_index = lax.axis_index("gc")
    row_windows = NWIN // grid_rows
    col_windows = NWIN // grid_cols
    local_rows = N // grid_rows
    local_cols = N // grid_cols
    scaled = (jnp.sqrt(row_scale)[:, :, None] * border.astype(jnp.float32)).astype(jnp.bfloat16)
    here, depth, width = scaled.shape
    pieces = PIECES if grid_cols <= 4 else 1
    rows, cols, head = gather(
        scaled.reshape(here * pieces, depth // pieces, width), grid_rows, grid_cols
    )
    rows = rows.reshape(-1, depth, width)
    cols = cols.reshape(-1, rows.shape[0], depth, width)
    head = head.reshape(-1, depth, BLK)
    row_pick = lax.dynamic_slice_in_dim(block_pick, row_index * row_windows, row_windows, 1)
    col_pick = lax.dynamic_slice_in_dim(block_pick, col_index * col_windows, col_windows, 1)
    roots = grid_rows // grid_cols
    own_stream = row_index - col_index * roots
    place = jnp.stack(
        [
            row_index * local_rows,
            col_index * local_cols,
            own_stream,
            (row_index == 0).astype(jnp.int32),
        ]
    ).astype(jnp.int32)
    diag_cols = lax.dynamic_slice_in_dim(given_diag, col_index * local_cols, local_cols, 0)
    return finish(
        place, row_pick, col_pick, block_pick[:, 0], rows, cols, head,
        given_diag[:HEAD], diag_cols, local_rows, local_cols,
    )


def solution(mesh):
    in_specs = (P("gc", None, "gr"), P("gc", None), P(), P())
    out_specs = P("gr", "gc")
    return jax.shard_map(body, mesh=mesh, in_specs=in_specs, out_specs=out_specs, check_vma=False)
```

```python
import functools

import jax
import jax.numpy as jnp
from jax import lax
from jax.experimental import pallas as pl
from jax.experimental.pallas import tpu as pltpu
from jax.sharding import PartitionSpec as P

N = 8192
BLK = 128
NWIN = 16
WSPAN = 4
HEAD = 512
MESH = pl.DeviceIdType.MESH
LAG = 2


def ring_swap(p):
    return p + ((p // 2) % 2) * (1 - 2 * (p % 2))


def gather_kernel(dims, scaled, rows, cols, head, own_sem, zrecv, zsend, recv, rsend, ssend):
    grid_rows, grid_cols, roots, parts, group = dims
    chips = grid_rows // 2
    units = grid_cols * parts
    me = lax.axis_index("gr")
    z = lax.axis_index("gc")
    core = lax.rem(me, 2)
    pos = ring_swap(me // 2)
    sibling = me + 1 - 2 * core
    ahead = ring_swap(lax.rem(pos + 1, chips)) * 2 + core
    behind = ring_swap(lax.rem(pos + chips - 1, chips)) * 2 + core
    has_up = z < grid_cols - 1
    has_down = z > 0

    barrier = pltpu.get_barrier_semaphore()
    for other in (sibling, ahead, behind):
        pl.semaphore_signal(barrier, inc=1, device_id=(other, z), device_id_type=MESH)

    @pl.when(has_up)
    def _():
        pl.semaphore_signal(barrier, inc=1, device_id=(me, z + 1), device_id_type=MESH)

    @pl.when(has_down)
    def _():
        pl.semaphore_signal(barrier, inc=1, device_id=(me, z - 1), device_id_type=MESH)

    own = pltpu.make_async_copy(
        scaled, rows.at[pl.ds(z * parts * group, parts * group)], own_sem
    )
    own.start()
    pl.semaphore_wait(barrier, 3 + has_up.astype(jnp.int32) + has_down.astype(jnp.int32))
    def mine(s):
        return scaled.at[pl.ds(s * group, group)]

    def zcopy(unit, up, src=None):
        where = pl.ds(unit * group, group)
        return pltpu.make_async_remote_copy(
            src_ref=rows.at[where] if src is None else src,
            dst_ref=rows.at[where],
            send_sem=zsend.at[1 if up else 0, unit],
            recv_sem=zrecv.at[unit],
            device_id=(me, z + 1 if up else z - 1),
            device_id_type=MESH,
        )

    def target(k, unit):
        where = pl.ds(unit * group, group)
        return head.at[where] if k == roots else cols.at[k, where]

    def narrow(k, ref):
        return ref.at[:, :, pl.ds(0, BLK)] if k == roots else ref

    def ring_copy(k, unit, src, forward):
        return pltpu.make_async_remote_copy(
            src_ref=src,
            dst_ref=target(k, unit),
            send_sem=rsend.at[k, unit],
            recv_sem=recv.at[k, unit],
            device_id=(ahead if forward else behind, z),
            device_id_type=MESH,
        )

    def sibling_copy(k, unit, src):
        return pltpu.make_async_remote_copy(
            src_ref=src,
            dst_ref=target(k, unit),
            send_sem=ssend.at[k, unit],
            recv_sem=recv.at[k, unit],
            device_id=(sibling, z),
            device_id_type=MESH,
        )

    def stream(k):
        root = z * roots + k if k < roots else 0 * z
        on_ring = core == lax.rem(root, 2)
        d = lax.rem(pos - ring_swap(root // 2) + chips, chips)
        return on_ring, d, lax.rem(chips - d, chips)

    streams = [stream(k) for k in range(roots + 1)]

    def send_along(k, unit, hop, forward, own_part):
        def both(src):
            ring_copy(k, unit, src, forward).start()
            sibling_copy(k, unit, src).start()

        @pl.when(hop == 0)
        def _():
            here = unit // parts == z

            @pl.when(here)
            def _():
                both(narrow(k, mine(own_part)))

            @pl.when(jnp.logical_not(here))
            def _():
                both(narrow(k, rows.at[pl.ds(unit * group, group)]))

        @pl.when(hop > 0)
        def _():
            ring_copy(k, unit, target(k, unit), forward).wait_recv()

            @pl.when(hop < chips - 1)
            def _():
                ring_copy(k, unit, target(k, unit), forward).start()

            sibling_copy(k, unit, target(k, unit)).start()

    def step(i, carry):
        t, s = i // parts, lax.rem(i, parts)
        low, high = z - t, z + t

        @pl.when(t == 0)
        def _():
            @pl.when(has_up)
            def _():
                zcopy(z * parts + s, True, mine(s)).start()

            @pl.when(has_down)
            def _():
                zcopy(z * parts + s, False, mine(s)).start()

        later = jnp.logical_and(t > 0, t < grid_cols)

        @pl.when(jnp.logical_and(later, low >= 0))
        def _():
            zcopy(low * parts + s, True).wait_recv()

            @pl.when(has_up)
            def _():
                zcopy(low * parts + s, True).start()

        @pl.when(jnp.logical_and(later, high < grid_cols))
        def _():
            zcopy(high * parts + s, False).wait_recv()

            @pl.when(has_down)
            def _():
                zcopy(high * parts + s, False).start()

        for forward in (True, False):
            for k in range(roots + 1):
                on_ring, d_ahead, d_behind = streams[k]
                hop = d_ahead if forward else d_behind
                slot = i - LAG * hop
                t2, s2 = slot // parts, lax.rem(slot, parts)
                good = jnp.logical_and(slot >= 0, slot < units)
                good = jnp.logical_and(good, lax.rem(slot + 2 * units, 2) == (0 if forward else 1))
                good = jnp.logical_and(good, on_ring)

                @pl.when(jnp.logical_and(good, z - t2 >= 0))
                def _():
                    send_along(k, (z - t2) * parts + s2, hop, forward, s2)

                other = jnp.logical_and(t2 > 0, z + t2 < grid_cols)

                @pl.when(jnp.logical_and(good, other))
                def _():
                    send_along(k, (z + t2) * parts + s2, hop, forward, s2)

        return carry

    lax.fori_loop(0, units + LAG * (chips - 1), step, 0)

    def finish(unit, carry):
        c, s = unit // parts, lax.rem(unit, parts)

        @pl.when(jnp.logical_and(c <= z, has_up))
        def _():
            zcopy(unit, True).wait_send()

        @pl.when(jnp.logical_and(c >= z, has_down))
        def _():
            zcopy(unit, False).wait_send()

        slot = jnp.where(c > z, c - z, z - c) * parts + s
        even = lax.rem(slot, 2) == 0
        for k in range(roots + 1):
            on_ring, d_ahead, d_behind = streams[k]
            hop = jnp.where(even, d_ahead, d_behind)

            @pl.when(on_ring)
            def _():
                @pl.when(hop < chips - 1)
                def _():
                    ring_copy(k, unit, target(k, unit), True).wait_send()

                sibling_copy(k, unit, target(k, unit)).wait_send()

            @pl.when(jnp.logical_not(on_ring))
            def _():
                sibling_copy(k, unit, target(k, unit)).wait_recv()

        return carry

    lax.fori_loop(0, units, finish, 0)
    own.wait()


def gather(scaled, grid_rows, grid_cols):
    here, depth, width = scaled.shape
    roots = grid_rows // grid_cols
    parts = here if grid_cols <= 4 else 1
    group = here // parts
    units = grid_cols * parts
    total = here * grid_cols
    dims = (grid_rows, grid_cols, roots, parts, group)
    dma = pltpu.SemaphoreType.DMA
    return pl.pallas_call(
        functools.partial(gather_kernel, dims),
        out_shape=(
            jax.ShapeDtypeStruct((total, depth, width), scaled.dtype),
            jax.ShapeDtypeStruct((roots, total, depth, width), scaled.dtype),
            jax.ShapeDtypeStruct((total, depth, BLK), scaled.dtype),
        ),
        in_specs=[pl.BlockSpec(memory_space=pl.ANY)],
        out_specs=[pl.BlockSpec(memory_space=pl.ANY)] * 3,
        scratch_shapes=[
            dma,
            dma((units,)),
            dma((2, units)),
            dma((roots + 1, units)),
            dma((roots + 1, units)),
            dma((roots + 1, units)),
        ],
        compiler_params=pltpu.CompilerParams(collective_id=0, has_side_effects=True),
        name="gather",
    )(scaled)


def full_dot(a, b, dims):
    return lax.dot_general(
        a, b, (dims, ((), ())), precision=lax.Precision.HIGHEST, preferred_element_type=jnp.float32
    )


def split(x):
    high = x.astype(jnp.bfloat16)
    return high, (x - high.astype(jnp.float32)).astype(jnp.bfloat16)


def three_dot(a, b, dims):
    dot = functools.partial(
        lax.dot_general, dimension_numbers=(dims, ((), ())), preferred_element_type=jnp.float32
    )
    return dot(a[0], b[0]) + (dot(a[0], b[1]) + dot(a[1], b[0]))


STEP = 4


def eliminate(jj, aug):
    rb = lax.broadcasted_iota(jnp.int32, (BLK, BLK), 0)
    cb = lax.broadcasted_iota(jnp.int32, (BLK, BLK), 1)
    lane = lax.broadcasted_iota(jnp.int32, (1, BLK), 1)
    j = jj * STEP
    block = aug[...]
    rows = [aug[pl.ds(j + a, 1), :] for a in range(STEP)]
    pick = lambda x, at, n: jnp.sum(jnp.where(at == n, x, 0.0), axis=1, keepdims=True)
    cols = [pick(block[:, :BLK], cb, j + a) for a in range(STEP)]
    low = [[None] * STEP for _ in range(STEP)]
    inv = [None] * STEP
    for a in range(STEP):
        for b in range(a + 1):
            v = pick(rows[b][:, :BLK], lane, j + a)
            for c in range(b):
                v = v - low[b][c] * low[a][c]
            if a == b:
                inv[a] = lax.rsqrt(v)
            else:
                low[a][b] = v * inv[b]
    done = rb[:, :1]
    units, factors = [], []
    for a in range(STEP):
        u, f = rows[a], cols[a]
        for b in range(a):
            u = u - low[a][b] * units[b]
            f = f - low[a][b] * factors[b]
        units.append(u * inv[a])
        factors.append(f * inv[a])
    for a in range(STEP):
        block = block - jnp.where(done >= j + STEP, factors[a], 0.0) * units[a]
    aug[...] = block
    for a in range(STEP):
        aug[pl.ds(j + a, 1), :] = units[a]


def factor(work, lower, inverse, aug):
    blocks = HEAD // BLK
    lower[...] = jnp.zeros_like(lower)
    inverse[...] = jnp.zeros_like(inverse)
    rb = lax.broadcasted_iota(jnp.int32, (BLK, BLK), 0)
    cb = lax.broadcasted_iota(jnp.int32, (BLK, BLK), 1)
    for kb in range(blocks):
        lo, hi = kb * BLK, (kb + 1) * BLK
        aug[:, :BLK] = work[lo:hi, lo:hi]
        aug[:, BLK:] = jnp.where(rb == cb, 1.0, 0.0)

        def turn(jj, carry):
            eliminate(jj, aug)
            return carry

        lax.fori_loop(0, BLK // STEP, turn, 0)
        upper = jnp.where(cb >= rb, aug[:, :BLK], 0.0)
        inv = jnp.where(cb <= rb, aug[:, BLK:], 0.0)
        lower[lo:hi, lo:hi] = upper.T
        inverse[lo:hi, lo:hi] = inv
        if hi < HEAD:
            below = full_dot(work[hi:, lo:hi], inv, ((1,), (1,)))
            lower[hi:, lo:hi] = below
            work[hi:, hi:] = work[hi:, hi:] - full_dot(below, below, ((1,), (1,)))
        if kb > 0:
            mix = full_dot(lower[lo:hi, :lo], inverse[:lo, :lo], ((1,), (0,)))
            inverse[lo:hi, :lo] = -full_dot(inv, mix, ((1,), (0,)))


def finish_kernel(
    roots, place, row_pick, col_pick, head_pick, rows, cols, head, diag_head, diag_cols, out,
    left, top, corner, lower, inverse, aug, lhs, rhs, top_high, top_low,
):
    s = pl.program_id(0)
    row_zero, col_zero, own_stream, own_head = place[0], place[1], place[2], place[3]
    width = rows.shape[2]
    row_wins = width // BLK

    @pl.when(s == 0)
    def _():
        out[...] = jnp.zeros_like(out)
        left[...] = jnp.zeros_like(left)
        top[...] = jnp.zeros_like(top)
        r = lax.broadcasted_iota(jnp.int32, (HEAD, HEAD), 0)
        c = lax.broadcasted_iota(jnp.int32, (HEAD, HEAD), 1)
        corner[...] = jnp.where(r == c, diag_head[...], 0.0)

    lhs[:, :width] = rows[0]
    for k in range(roots):
        part = slice(k * width, (k + 1) * width)

        @pl.when(own_stream == k)
        def _():
            rhs[:, part] = rows[0]

        @pl.when(own_stream != k)
        def _():
            rhs[:, part] = cols[k, 0]

    @pl.when(own_head == 1)
    def _():
        lhs[:, width:] = rows[0, :, :BLK]
        rhs[:, roots * width :] = rows[0, :, :BLK]

    @pl.when(own_head == 0)
    def _():
        lhs[:, width:] = head[0]
        rhs[:, roots * width :] = head[0]

    gram = lax.dot_general(
        lhs[...], rhs[...], (((0,), (0,)), ((), ())), preferred_element_type=jnp.float32
    )

    def spot(win, pick):
        return pl.ds(pl.multiple_of(win * WSPAN * BLK + pick * BLK, BLK), BLK)

    at_head = spot(0, head_pick[s])
    cut = lambda a, b: gram[a * BLK : (a + 1) * BLK, b * BLK : (b + 1) * BLK]
    col_wins = roots * row_wins
    corner[at_head, at_head] += cut(row_wins, col_wins)
    for a in range(row_wins):
        left[spot(a, row_pick[s, a]), at_head] += cut(a, col_wins)
    for b in range(col_wins):
        here = spot(b, col_pick[s, b])
        top[at_head, here] += cut(row_wins, b)
        for a in range(row_wins):
            out[spot(a, row_pick[s, a]), here] += cut(a, b)

    @pl.when(s == pl.num_programs(0) - 1)
    def _():
        factor(corner, lower, inverse, aug)
        inv = split(inverse[...])
        n_rows, n_cols = out.shape
        wide = 512
        for c in range(n_cols // wide):
            at = slice(c * wide, (c + 1) * wide)
            top_high[:, at], top_low[:, at] = split(
                three_dot(inv, split(top[:, at]), ((1,), (0,)))
            )
        tile = 256

        def strip(i, carry):
            at = pl.ds(pl.multiple_of(i * tile, tile), tile)
            panel = three_dot(split(left[at, :]), inv, ((1,), (1,)))
            first = row_zero + i * tile

            @pl.when(first >= HEAD)
            def _():
                product = three_dot(split(panel), (top_high[...], top_low[...]), ((1,), (0,)))
                r = first + lax.broadcasted_iota(jnp.int32, (tile, n_cols), 0)
                c = col_zero + lax.broadcasted_iota(jnp.int32, (tile, n_cols), 1)
                out[at, :] = out[at, :] + jnp.where(r == c, diag_cols[...], 0.0) - product

                @pl.when(col_zero == 0)
                def _():
                    out[at, :HEAD] = panel

            @pl.when(first < HEAD)
            def _():
                out[at, :] = jnp.zeros((tile, n_cols), jnp.float32)

                @pl.when(col_zero == 0)
                def _():
                    out[at, :HEAD] = lower[pl.ds(pl.multiple_of(first, tile), tile), :]

            return carry

        lax.fori_loop(0, n_rows // tile, strip, 0)


def finish(place, row_pick, col_pick, head_pick, rows, cols, head, diag_head, diag_cols, n_rows, n_cols):
    total, depth, width = rows.shape
    roots = cols.shape[0]
    f32, bf16 = jnp.float32, jnp.bfloat16
    whole = lambda s, *_: (0, 0)
    grid_spec = pltpu.PrefetchScalarGridSpec(
        num_scalar_prefetch=4,
        grid=(total,),
        in_specs=[
            pl.BlockSpec((1, depth, width), lambda s, *_: (s, 0, 0)),
            pl.BlockSpec((roots, 1, depth, width), lambda s, *_: (0, s, 0, 0)),
            pl.BlockSpec((1, depth, BLK), lambda s, *_: (s, 0, 0)),
            pl.BlockSpec((1, HEAD), whole),
            pl.BlockSpec((1, n_cols), whole),
        ],
        out_specs=pl.BlockSpec((n_rows, n_cols), whole),
        scratch_shapes=[
            pltpu.VMEM((n_rows, HEAD), f32),
            pltpu.VMEM((HEAD, n_cols), f32),
            pltpu.VMEM((HEAD, HEAD), f32),
            pltpu.VMEM((HEAD, HEAD), f32),
            pltpu.VMEM((HEAD, HEAD), f32),
            pltpu.VMEM((BLK, 2 * BLK), f32),
            pltpu.VMEM((depth, width + BLK), bf16),
            pltpu.VMEM((depth, roots * width + BLK), bf16),
            pltpu.VMEM((HEAD, n_cols), bf16),
            pltpu.VMEM((HEAD, n_cols), bf16),
        ],
    )
    return pl.pallas_call(
        functools.partial(finish_kernel, roots),
        grid_spec=grid_spec,
        out_shape=jax.ShapeDtypeStruct((n_rows, n_cols), f32),
        compiler_params=pltpu.CompilerParams(vmem_limit_bytes=56 * 1024 * 1024),
        name="finish",
    )(
        place, row_pick, col_pick, head_pick, rows, cols, head,
        diag_head.reshape(1, HEAD), diag_cols.reshape(1, n_cols),
    )


def body(border, row_scale, block_pick, given_diag):
    grid_rows = lax.axis_size("gr")
    grid_cols = lax.axis_size("gc")
    row_index = lax.axis_index("gr")
    col_index = lax.axis_index("gc")
    row_windows = NWIN // grid_rows
    col_windows = NWIN // grid_cols
    local_rows = N // grid_rows
    local_cols = N // grid_cols
    scaled = (jnp.sqrt(row_scale)[:, :, None] * border.astype(jnp.float32)).astype(jnp.bfloat16)
    rows, cols, head = gather(scaled, grid_rows, grid_cols)
    row_pick = lax.dynamic_slice_in_dim(block_pick, row_index * row_windows, row_windows, 1)
    col_pick = lax.dynamic_slice_in_dim(block_pick, col_index * col_windows, col_windows, 1)
    roots = grid_rows // grid_cols
    own_stream = row_index - col_index * roots
    place = jnp.stack(
        [
            row_index * local_rows,
            col_index * local_cols,
            own_stream,
            (row_index == 0).astype(jnp.int32),
        ]
    ).astype(jnp.int32)
    diag_cols = lax.dynamic_slice_in_dim(given_diag, col_index * local_cols, local_cols, 0)
    return finish(
        place, row_pick, col_pick, block_pick[:, 0], rows, cols, head,
        given_diag[:HEAD], diag_cols, local_rows, local_cols,
    )


def solution(mesh):
    in_specs = (P("gc", None, "gr"), P("gc", None), P(), P())
    out_specs = P("gr", "gc")
    return jax.shard_map(body, mesh=mesh, in_specs=in_specs, out_specs=out_specs, check_vma=False)
```
